512 devices in a mesh: prompt: 16 (over x, y_hi, core), comp: 32 (over z, y_lo).
Axes of the slice: x: 4, y: 4 (y_hi: 2, y_lo: 2; y = y_hi * 2 + y_lo), z: 16, core: 2. Of those that a mesh axis runs over, the one named last changes fastest.
Arguments:
- queries: bfloat16 [16384, 4096], P('comp', 'prompt'), may hold values from -128 to 128
- comp_kv: bfloat16 [2, 16384, 1024], P(None, 'comp'), may hold values from -8 to 8
- prompt_kv: bfloat16 [2, 8, 4096, 1024], P(None, None, 'prompt'), may hold values from -8 to 8
- comp_lengths: int32 [2, 16], replicated, may hold values from 1 to 1024, 8192 in all within a row
- group_prompt: int32 [2], replicated, may hold values from 0 to 7
Outputs:
- attended: bfloat16 [16384, 4096], P('comp', 'prompt')
The draws below stay inside these ranges and needn't reach their ends.
Inputs may be any that keep to these rules, and one draw needn't show every extreme that they name: `comp_lengths`: the 16 lengths of each group sum to 8192, and the longest of each group is exactly 1024.
All inputs are finite; a program needn't handle non-finite values.
Results may differ from the reference program's by a relative error of at most 0.009.
Values may be sent and summed in bfloat16 or wider, within the bound.
A program may use at most 128 MiB of HBM per device.

```python
import math
import jax
import jax.numpy as jnp
import numpy as np
from jax import lax

HEADS = 32
KV_HEADS = 8
HD = 128
COMPS = 16
GROUPS = 2
PROMPTS = 8
ROWS_DEV = 512
CTOK = 16384
PLEN = 4096
GROUP_TOK = 8192
LONGEST = 1024
N_COMP = 32


def shared_keys(key):
    return jax.random.normal(key, (CTOK, KV_HEADS * HD), jnp.float32)


def draw_queries(key, part):
    key = jax.random.fold_in(key, 5)
    noise_key = jax.random.fold_in(key, 0)
    drawn_draw = jax.random.normal(noise_key, (CTOK, HEADS * HD), jnp.float32)
    return jnp.clip(drawn_draw, -128.0, 128.0).astype(jnp.bfloat16)


def draw_comp_kv(key, part):
    shared = shared_keys(key)
    key = jax.random.fold_in(key, 11)
    value_key = jax.random.fold_in(key, 0)
    values_drawn = jax.random.normal(value_key, (CTOK, KV_HEADS * HD), jnp.float32)
    keys_drawn = shared
    return jnp.clip(jnp.stack([keys_drawn, values_drawn]), -8.0, 8.0).astype(jnp.bfloat16)


def steps_of(key, extent, shards, least, top_value):
    loudness = 1.0
    for position, shards_of in shards:
        heights = jax.random.uniform(jax.random.fold_in(jax.random.fold_in(key, 6), position), (shards_of,), jnp.float32, least / len(shards), top_value / len(shards))
        loudness = loudness * jnp.repeat(jnp.exp(heights), extent[position] // shards_of).reshape((-1,) + (1,) * (len(extent) - 1 - position))
    return loudness


def split_up(amount, total, limit, lean):
    loads = [(1 << 20) // math.isqrt(rank ** lean) + 1 for rank in range(2, amount + 1)]
    rest, counts = total - limit - (amount - 1), [1] * (amount - 1)
    while rest > 0:
        candidates = [i for i in range(amount - 1) if counts[i] < limit]
        pool, budget = sum([loads[i] for i in candidates]), rest
        for i in candidates:
            extra = min(limit - counts[i], max(1, budget * loads[i] // pool), rest)
            counts[i] = counts[i] + extra
            rest = rest - extra
    return np.array([limit] + counts)


def uneven(rng, count, total, most, skew):
    if count == 2:
        one = jax.random.randint(rng, (), max(1, total - most), min(most, total - 1) + 1)
        return jnp.stack([one, total - one])
    tallies = jnp.asarray(split_up(count, total, most, skew), jnp.int32)
    pairs = (count - 1) // 2
    source_of, sink = tallies[1:1 + 2 * pairs:2], tallies[2:2 + 2 * pairs:2]
    slack = jnp.minimum(source_of - 1, most - sink)
    moved = jax.random.randint(jax.random.fold_in(rng, 1), (pairs,), 0, 1 << 20) % (slack + 1)
    tallies = tallies.at[1:1 + 2 * pairs:2].set(source_of - moved).at[2:2 + 2 * pairs:2].set(sink + moved)
    return tallies[jax.random.permutation(jax.random.fold_in(rng, 2), count)]


def normal_values(rng, extent, spread, most, cuts=(), held_as=jnp.bfloat16):
    entries = jax.random.normal(rng, extent, jnp.float32) * spread
    if len(cuts) > 0:
        entries = steps_of(rng, extent, cuts, -0.22, 0.18) * entries
    return jnp.clip(entries, min=-most, max=most).astype(held_as)


def setup_inputs(seed: int = 0) -> dict:
    arg_keys = jax.random.split(jax.random.key(seed), 6)
    queries = draw_queries(jax.random.fold_in(arg_keys[5], 71), 0)
    comp_kv = draw_comp_kv(jax.random.fold_in(arg_keys[5], 71), 0)
    prompt_kv = normal_values(arg_keys[2], (2, PROMPTS, PLEN, KV_HEADS * HD), 1.0, 8.0, ((2, 16),))
    comp_lengths = jax.vmap(lambda own: uneven(own, COMPS, GROUP_TOK, LONGEST, 2))(jax.random.split(arg_keys[3], GROUPS)).reshape((GROUPS, COMPS)).astype(jnp.int32)
    group_prompt = jax.random.randint(arg_keys[4], (GROUPS,), 0, PROMPTS).astype(jnp.int32)
    return {"queries": queries, "comp_kv": comp_kv, "prompt_kv": prompt_kv, "comp_lengths": comp_lengths, "group_prompt": group_prompt}


def completion_ids(comp_lengths, row_ids, group_tok):
    clamped = jnp.maximum(row_ids, 0)
    group_index = clamped // group_tok
    offset = clamped - group_index * group_tok
    group_ends = jnp.cumsum(comp_lengths, axis=1).astype(jnp.int32)
    group_list = jnp.arange(comp_lengths.shape[0], dtype=jnp.int32)
    matches = (group_list[None, :, None] == group_index[:, None, None]) & (group_ends[None, :, :] <= offset[:, None, None])
    return group_index * comp_lengths.shape[1] + lax.optimization_barrier(jnp.sum(matches.astype(jnp.int32), axis=(1, 2)))

def head_scores(grouped, key_heads):
    return jnp.einsum('rkgd,nkd->rkgn', grouped.astype(jnp.float32), key_heads.astype(jnp.float32)) / math.sqrt(HD)

def weighted_values(weights, value_heads):
    rounded = lax.optimization_barrier(weights.astype(jnp.bfloat16))
    return jnp.einsum('rkgn,nkd->rkgd', rounded.astype(jnp.float32), value_heads.astype(jnp.float32))

def reference(queries, comp_kv, prompt_kv, comp_lengths, group_prompt):
    group_tok = CTOK // GROUPS
    share_count = HEADS // KV_HEADS
    padded = jnp.concatenate([jnp.zeros((2, 2 * ROWS_DEV, KV_HEADS * HD), comp_kv.dtype), comp_kv], axis=1)

    def one_block(block_index):
        first_row = (block_index * ROWS_DEV).astype(jnp.int32)
        rows_here = first_row + jnp.arange(ROWS_DEV, dtype=jnp.int32)
        key_rows = first_row - 2 * ROWS_DEV + jnp.arange(3 * ROWS_DEV, dtype=jnp.int32)
        grouped = lax.dynamic_slice_in_dim(queries, first_row, ROWS_DEV, 0).reshape(ROWS_DEV, KV_HEADS, share_count, HD)
        prompt_id = lax.dynamic_index_in_dim(group_prompt, (first_row // group_tok).astype(jnp.int32), 0, keepdims=False)
        prompt_pair = lax.dynamic_index_in_dim(prompt_kv, prompt_id.astype(jnp.int32), 1, keepdims=False)
        comp_pair = lax.dynamic_slice_in_dim(padded, first_row, 3 * ROWS_DEV, 1)
        seg_rows = completion_ids(comp_lengths, rows_here, group_tok)
        seg_keys = completion_ids(comp_lengths, key_rows, group_tok)
        visible = (seg_rows[:, None] == seg_keys[None, :]) & (key_rows[None, :] <= rows_here[:, None]) & (key_rows[None, :] >= 0)
        prefix_scores = head_scores(grouped, prompt_pair[0].reshape(PLEN, KV_HEADS, HD))
        suffix_scores = head_scores(grouped, comp_pair[0].reshape(3 * ROWS_DEV, KV_HEADS, HD))
        suffix_scores = jnp.where(visible[:, None, None, :], suffix_scores, -jnp.inf)
        row_max = jnp.maximum(lax.optimization_barrier(jnp.max(prefix_scores, axis=-1)), lax.optimization_barrier(jnp.max(suffix_scores, axis=-1)))
        prefix_weights = jnp.exp(prefix_scores - row_max[..., None])
        suffix_weights = jnp.exp(suffix_scores - row_max[..., None])
        denominator = lax.optimization_barrier(jnp.sum(prefix_weights, axis=-1)) + lax.optimization_barrier(jnp.sum(suffix_weights, axis=-1))
        numerator = weighted_values(prefix_weights, prompt_pair[1].reshape(PLEN, KV_HEADS, HD))
        numerator = numerator + weighted_values(suffix_weights, comp_pair[1].reshape(3 * ROWS_DEV, KV_HEADS, HD))
        return (numerator / denominator[..., None]).reshape(ROWS_DEV, HEADS * HD).astype(jnp.bfloat16)
    outputs = lax.map(one_block, jnp.arange(N_COMP, dtype=jnp.int32))
    return outputs.reshape(CTOK, HEADS * HD)
```

```python
import functools
import math

import jax
import jax.numpy as jnp
from jax import lax
from jax.experimental import pallas as pl
from jax.experimental.pallas import tpu as pltpu
from jax.sharding import PartitionSpec as P

HEADS = 32
KV_HEADS = 8
HD = 128
ROWS = 512
TOK = 256
HALF = 128
HERE = 2
PER_GROUP = 16
SCALE = math.log2(math.e) / math.sqrt(HD)
MESH = pl.DeviceIdType.MESH
MOVES = ((1, 0), (3, 0), (0, 1), (1, 1), (3, 1), (2, 0), (2, 1))
N_MSG = len(MOVES)


def kernel(
    q_hbm, comp_hbm, prompt_hbm, lengths_hbm, group_prompt_hbm, out_ref,
    lengths, group_prompt, q_buf, stage_0, stage_1, stage_2, stage_3, stage_4, stage_5, stage_6, stage_7, stage_8, sbuf, cbuf, pbuf, qt, acc, m_s, l_s,
    small_sem, q_sem, own_sem, stage_sem,
    up_send, up_recv, lo_send, lo_recv, sibc_send, sibc_recv,
    dir_send, dir_recv, par_send, par_recv, sib_send, sib_recv,
):
    p, c = lax.axis_index("prompt"), lax.axis_index("comp")
    x, h, co = p // 4, (p // 2) % 2, p % 2
    z, lo = c // 2, c % 2
    zg = z % 8
    group = c // PER_GROUP
    head = p // 2
    sibling = (p + 1 - 2 * co, c)
    lo_partner = (p, c + 1 - 2 * lo)
    z_partner = (p, c + 2 - 4 * (z % 2))
    partner = (p, c + (1 - co) * (1 - 2 * lo) + co * (2 - 4 * (z % 2)))

    def at(dx, dh):
        return ((x + dx + 4) % 4) * 4 + ((h + dh) % 2) * 2 + co, z * 2 + (lo + dh) % 2

    stage = [stage_0, stage_1, stage_2, stage_3, stage_4, stage_5, stage_6, stage_7, stage_8]

    small = [
        pltpu.make_async_copy(lengths_hbm, lengths, small_sem.at[0]),
        pltpu.make_async_copy(group_prompt_hbm, group_prompt, small_sem.at[1]),
    ]
    for copy in small:
        copy.start()
    q_copy = pltpu.make_async_copy(q_hbm, q_buf, q_sem)
    q_copy.start()
    own_copy = pltpu.make_async_copy(
        comp_hbm.at[:, :, pl.ds(pl.multiple_of(head * HD, HD), HD)], cbuf.at[0], own_sem
    )
    own_copy.start()
    loads = []
    for j in range(N_MSG + 2):
        if 1 <= j <= N_MSG:
            dx, dh = MOVES[j - 1]
            to_head = at(dx, dh)[0] // 2
            half = (z + (lo + dh) % 2) % 2
        else:
            to_head, half = head, j // (N_MSG + 1)
        copy = pltpu.make_async_copy(
            prompt_hbm.at[
                :,
                :,
                pl.ds(pl.multiple_of(half * HALF, HALF), HALF),
                pl.ds(pl.multiple_of(to_head * HD, HD), HD),
            ],
            stage[j],
            stage_sem.at[j],
        )
        loads.append(copy)
    for j in list(range(1, N_MSG + 1)) + [0, N_MSG + 1]:
        loads[j].start()

    barrier = pltpu.get_barrier_semaphore()

    def tell(device):
        pl.semaphore_signal(barrier, inc=1, device_id=device, device_id_type=MESH)

    for dx, dh in MOVES:
        tell(at(-dx, dh))
    tell(sibling)
    tell(lo_partner)

    @pl.when(co == 1)
    def _():
        tell(z_partner)

    @pl.when(zg > 0)
    def _():
        tell((p, c - 2))

    q_copy.wait()
    for n in range(HERE):
        q = q_buf[:, n * HD : (n + 1) * HD].astype(jnp.float32) * SCALE
        q = q.T
        high = q.astype(jnp.bfloat16)
        qt[0:HD, n * ROWS : (n + 1) * ROWS] = high
        qt[HD : 2 * HD, n * ROWS : (n + 1) * ROWS] = (q - high.astype(jnp.float32)).astype(
            jnp.bfloat16
        )
    m_s[...] = jnp.full_like(m_s, -1e30)
    l_s[...] = jnp.zeros_like(l_s)
    acc[...] = jnp.zeros_like(acc)

    own_copy.wait()
    pl.semaphore_wait(barrier, 9 + co + (7 - zg + 6) // 7)

    def remote(src, dst, send, recv, device):
        return pltpu.make_async_remote_copy(
            src_ref=src, dst_ref=dst, send_sem=send, recv_sem=recv, device_id=device, device_id_type=MESH
        )

    up = remote(cbuf.at[0, co], cbuf.at[2, co], up_send, up_recv, (p, c + 2))

    @pl.when(zg < 7)
    def _():
        up.start()

    for copy in small:
        copy.wait()
    prompt_id = group_prompt[group]
    direct = []
    for j in range(1, N_MSG + 1):
        loads[j].wait()
        for kv in range(2):
            sbuf[j - 1, kv] = stage[j][kv, prompt_id]
        copy = remote(sbuf.at[j - 1], pbuf.at[j, 0], dir_send.at[j], dir_recv.at[j], at(*MOVES[j - 1]))
        copy.start()
        direct.append(copy)
    for j, slot in ((0, 0), (N_MSG + 1, 1)):
        loads[j].wait()
        for kv in range(2):
            pbuf[0, slot, kv] = stage[j][kv, prompt_id]
    own_pair = remote(
        pbuf.at[0, pl.ds(0, 2)], pbuf.at[0, pl.ds(2, 2)], sib_send.at[0, 0], sib_recv.at[0, 0], sibling
    )
    own_pair.start()

    lane = lax.broadcasted_iota(jnp.int32, (1, ROWS), 1)
    base = (c % PER_GROUP) * ROWS
    offset = lane + base
    first = jnp.zeros_like(offset)
    end = jnp.int32(0)
    for n in range(lengths.shape[1]):
        end = end + lengths[group, n]
        first = jnp.where(offset >= end, end, first)
    first = first - base

    def attend(keys, values, distance):
        pair = jnp.concatenate([keys, keys], axis=1)
        if distance is not None:
            key = lax.broadcasted_iota(jnp.int32, (ROWS, ROWS), 0)
            seen = (key >= first + distance * ROWS) & (key <= lane + distance * ROWS)
        scores = []
        for n in range(HERE):
            scores.append(
                jnp.dot(
                    pair, qt[:, n * ROWS : (n + 1) * ROWS], preferred_element_type=jnp.float32
                )
            )
        for n in range(HERE):
            s, cols = scores[n], slice(n * ROWS, (n + 1) * ROWS)
            if distance is not None:
                s = jnp.where(seen, s, -1e30)
            old = m_s[:, cols]
            top = jnp.maximum(old, jnp.max(s, axis=0, keepdims=True))
            decay = jnp.exp2(old - top)
            weights = jnp.exp2(s - top)
            l_s[:, cols] = l_s[:, cols] * decay + jnp.sum(weights, axis=0, keepdims=True)
            m_s[:, cols] = top
            part = lax.dot_general(
                values,
                weights.astype(jnp.bfloat16),
                (((0,), (0,)), ((), ())),
                preferred_element_type=jnp.float32,
            )
            acc[:, cols] = acc[:, cols] * decay + part

    def attend_comp(slot, distance):
        attend(cbuf[slot, 0], cbuf[slot, 1], distance)

    def attend_prompt(j):
        attend(pbuf[j, :, 0].reshape(4 * HALF, HD), pbuf[j, :, 1].reshape(4 * HALF, HD), None)

    attend_comp(0, 0)

    @pl.when(zg > 0)
    def _():
        up.wait_recv()

    @pl.when(zg == 0)
    def _():
        cbuf[2, co] = jnp.zeros((ROWS, HD), jnp.bfloat16)

    across = remote(cbuf.at[2 * lo, co], cbuf.at[1, co], lo_send, lo_recv, lo_partner)
    across.start()
    far = remote(cbuf.at[2, co], cbuf.at[2, co], sibc_send.at[0], sibc_recv.at[0], sibling)
    far.start()

    own_pair.wait_recv()
    attend_prompt(0)

    across.wait_recv()
    near = remote(cbuf.at[1, co], cbuf.at[1, co], sibc_send.at[1], sibc_recv.at[1], sibling)
    near.start()

    def to_partner(j):
        return remote(pbuf.at[j, 0], pbuf.at[j, 2], par_send.at[j], par_recv.at[j], partner)

    def to_sibling(j, slot):
        return remote(
            pbuf.at[j, slot],
            pbuf.at[j, slot + 1],
            sib_send.at[j, slot // 2],
            sib_recv.at[j, slot // 2],
            sibling,
        )

    def serve_direct(j):
        remote(sbuf.at[j - 1], pbuf.at[j, 0], dir_send.at[j], dir_recv.at[j], sibling).wait_recv()
        to_partner(j).start()
        to_sibling(j, 0).start()

    def serve_partner(j):
        to_partner(j).wait_recv()
        to_sibling(j, 2).start()

    serve_direct(1)
    far.wait_recv()
    attend_comp(2, 2)
    serve_direct(2)
    serve_partner(1)
    near.wait_recv()
    attend_comp(1, 1)

    def step(j, carry):
        @pl.when(j <= N_MSG - 2)
        def _():
            serve_direct(j + 2)

        @pl.when(j <= N_MSG - 1)
        def _():
            serve_partner(j + 1)

        to_sibling(j, 0).wait_recv()
        to_sibling(j, 2).wait_recv()
        attend_prompt(j)
        return carry

    lax.fori_loop(1, N_MSG + 1, step, 0)

    for n in range(HERE):
        cols = slice(n * ROWS, (n + 1) * ROWS)
        out = acc[:, cols] / l_s[:, cols]
        out_ref[:, n * HD : (n + 1) * HD] = out.T.astype(jnp.bfloat16)

    @pl.when(zg < 7)
    def _():
        up.wait_send()

    across.wait_send()
    far.wait_send()
    near.wait_send()
    own_pair.wait_send()
    for copy in direct:
        copy.wait_send()

    def drain(j, carry):
        to_partner(j).wait_send()
        to_sibling(j, 0).wait_send()
        to_sibling(j, 2).wait_send()
        return carry

    lax.fori_loop(1, N_MSG + 1, drain, 0)


def body(queries, comp_kv, prompt_kv, comp_lengths, group_prompt):
    bf16 = jnp.bfloat16
    dma = pltpu.SemaphoreType.DMA
    return pl.pallas_call(
        kernel,
        out_shape=jax.ShapeDtypeStruct((ROWS, HERE * HD), bf16),
        in_specs=[pl.BlockSpec(memory_space=pltpu.HBM)] * 5,
        out_specs=pl.BlockSpec(memory_space=pltpu.VMEM),
        scratch_shapes=[
            pltpu.SMEM((2, PER_GROUP), jnp.int32),
            pltpu.SMEM((2,), jnp.int32),
            pltpu.VMEM((ROWS, HERE * HD), bf16),
            *[pltpu.VMEM((2, 8, HALF, HD), bf16) for _ in range(N_MSG + 2)],
            pltpu.VMEM((N_MSG, 2, HALF, HD), bf16),
            pltpu.VMEM((3, 2, ROWS, HD), bf16),
            pltpu.VMEM((N_MSG + 1, 4, 2, HALF, HD), bf16),
            pltpu.VMEM((2 * HD, HERE * ROWS), bf16),
            pltpu.VMEM((HD, HERE * ROWS), jnp.float32),
            pltpu.VMEM((1, HERE * ROWS), jnp.float32),
            pltpu.VMEM((1, HERE * ROWS), jnp.float32),
            dma((2,)),
            dma(()),
            dma(()),
            dma((N_MSG + 2,)),
            dma(()),
            dma(()),
            dma(()),
            dma(()),
            dma((2,)),
            dma((2,)),
            dma((N_MSG + 1,)),
            dma((N_MSG + 1,)),
            dma((N_MSG + 1,)),
            dma((N_MSG + 1,)),
            dma((N_MSG + 1, 2)),
            dma((N_MSG + 1, 2)),
        ],
        compiler_params=pltpu.CompilerParams(
            collective_id=0, has_side_effects=True, vmem_limit_bytes=48 * 2**20
        ),
        cost_estimate=pl.CostEstimate(
            flops=4 * 1024 * 5632 * HD, bytes_accessed=12 * 2**20, transcendentals=1024 * 5632
        ),
    )(*[pltpu.with_memory_space_constraint(a, pltpu.HBM) for a in (queries, comp_kv, prompt_kv, comp_lengths, group_prompt)])


def solution(mesh):
    placed = (P("comp", "prompt"), P(None, "comp", None), P(None, None, "prompt", None), P(), P())
    return jax.shard_map(
        body, mesh=mesh, in_specs=placed, out_specs=P("comp", "prompt"), check_vma=False
    )
```

```python
import functools
import math

import jax
import jax.numpy as jnp
from jax import lax
from jax.experimental import pallas as pl
from jax.experimental.pallas import tpu as pltpu
from jax.sharding import PartitionSpec as P

HEADS = 32
KV_HEADS = 8
HD = 128
ROWS = 512
TOK = 256
HALF = 128
HERE = 2
PER_GROUP = 16
SCALE = math.log2(math.e) / math.sqrt(HD)
MESH = pl.DeviceIdType.MESH
MOVES = ((1, 0), (3, 0), (0, 1), (1, 1), (3, 1), (2, 0), (2, 1))
N_MSG = len(MOVES)
FAR = 7
N_LOAD = N_MSG + 2 + N_MSG - FAR
ORDER = ("O", "D1", "D3", "C2", "D5", "C1", "P1", "P3", "P5", "N7")
AHEAD = ("O", "D1", "D3", "C2", "D5", "C1", "P1", "P3", "P5",)
SERVE = (
    (("D", 1), ("D", 2),),
    (("C", 2), ("D", 3), ("D", 4),),
    (("D", 5), ("P", 1), ("D", 6),),
    (("C", 1), ("P", 2), ("D", 7),),
    (("P", 3), ("P", 4),),
    (("P", 5),),
    (("P", 6),),
    (("P", 7),),
    (),
    (),
)
NEEDS = {
    "O": (("O", 0),),
    "D1": (("D", 1), ("D", 2)),
    "D3": (("D", 3), ("D", 4)),
    "P1": (("P", 1), ("P", 2)),
    "P3": (("P", 3), ("P", 4)),
    "D5": (("D", 5), ("D", 6)),
    "P5": (("P", 5), ("P", 6)),
    "N5": (("D", 5), ("P", 5)),
    "N6": (("D", 6), ("P", 6)),
    "N7": (("D", 7), ("P", 7)),
    "C1": (("C", 1),),
    "C2": (("C", 2),),
}


def kernel(
    q_hbm, comp_hbm, prompt_hbm, lengths_hbm, group_prompt_hbm, out_ref,
    lengths, group_prompt, sb, q_buf, stage_0, stage_1, stage_2, stage_3, stage_4, stage_5, stage_6, stage_7, stage_8, sbuf, cbuf, pbuf, qt, acc, m_s, l_s,
    small_sem, q_sem, own_sem, stage_sem,
    up_send, up_recv, sibc_send, sibc_recv,
    dir_send, dir_recv, par_send, par_recv, sib_send, sib_recv,
):
    p, c = lax.axis_index("prompt"), lax.axis_index("comp")
    x, h, co = p // 4, (p // 2) % 2, p % 2
    z, lo = c // 2, c % 2
    group = c // PER_GROUP
    head = p // 2
    sibling = (p + 1 - 2 * co, c)
    partner = (p, c + (1 - co) * (1 - 2 * lo) + co * (2 - 4 * (z % 2)))

    def at(dx, dh):
        return ((x + dx + 4) % 4) * 4 + ((h + dh) % 2) * 2 + co, z * 2 + (lo + dh) % 2

    stage = [stage_0, stage_1, stage_2, stage_3, stage_4, stage_5, stage_6, stage_7, stage_8]

    small = [
        pltpu.make_async_copy(lengths_hbm, lengths, small_sem.at[0]),
        pltpu.make_async_copy(group_prompt_hbm, group_prompt, small_sem.at[1]),
    ]
    for copy in small:
        copy.start()
    q_copy = pltpu.make_async_copy(q_hbm, q_buf, q_sem)
    q_copy.start()
    own_copy = pltpu.make_async_copy(
        comp_hbm.at[:, :, pl.ds(pl.multiple_of(head * HD, HD), HD)], cbuf.at[0], own_sem
    )
    own_copy.start()
    loads = []
    for j in range(N_LOAD):
        if j in (0, N_MSG + 1):
            to_head, half = head, j // (N_MSG + 1)
        else:
            second = j // (N_MSG + 1)
            dx, dh = MOVES[j - 1 if j <= N_MSG else j - (N_MSG + 2) + FAR]
            to_head = at(dx, dh)[0] // 2
            half = (z + (lo + dh) % 2 + second) % 2
        copy = pltpu.make_async_copy(
            prompt_hbm.at[
                :,
                :,
                pl.ds(pl.multiple_of(half * HALF, HALF), HALF),
                pl.ds(pl.multiple_of(to_head * HD, HD), HD),
            ],
            stage[j],
            stage_sem.at[j],
        )
        loads.append(copy)
    for j in list(range(1, N_MSG + 1)) + list(range(N_MSG + 2, N_LOAD)) + [0, N_MSG + 1]:
        loads[j].start()

    barrier = pltpu.get_barrier_semaphore()

    def tell(device):
        pl.semaphore_signal(barrier, inc=1, device_id=device, device_id_type=MESH)

    for dx, dh in MOVES:
        tell(at(-dx, dh))
    tell(sibling)
    tell(partner)
    for n in (1, 2):

        @pl.when(c % PER_GROUP >= n)
        def _():
            tell((p, c - n))

    q_copy.wait()
    for n in range(HERE):
        q = q_buf[:, n * HD : (n + 1) * HD].astype(jnp.float32) * SCALE
        q = q.T
        high = q.astype(jnp.bfloat16)
        qt[0:HD, n * ROWS : (n + 1) * ROWS] = high
        qt[HD : 2 * HD, n * ROWS : (n + 1) * ROWS] = (q - high.astype(jnp.float32)).astype(
            jnp.bfloat16
        )
    m_s[...] = jnp.full_like(m_s, -1e30)
    l_s[...] = jnp.zeros_like(l_s)
    acc[...] = jnp.zeros_like(acc)

    own_copy.wait()
    for copy in small:
        copy.wait()

    lane = lax.broadcasted_iota(jnp.int32, (1, ROWS), 1)
    base = (c % PER_GROUP) * ROWS
    offset = lane + base
    first = jnp.zeros_like(offset)
    end = jnp.int32(0)
    for n in range(lengths.shape[1]):
        end = end + lengths[group, n]
        first = jnp.where(offset >= end, end, first)
    first = first - base

    def first_scores(keys, n):
        return jnp.dot(
            jnp.concatenate([keys, keys], axis=1),
            qt[:, n * ROWS : (n + 1) * ROWS],
            preferred_element_type=jnp.float32,
        )

    def softmax_part(s, n, values, distance):
        cols = slice(n * ROWS, (n + 1) * ROWS)
        if distance is not None:
            key = lax.broadcasted_iota(jnp.int32, (ROWS, ROWS), 0)
            seen = key >= first + distance * ROWS
            if distance == 0:
                seen = seen & (key <= lane)
            s = jnp.where(seen, s, -1e30)
        old = m_s[:, cols]
        top = jnp.maximum(old, jnp.max(s, axis=0, keepdims=True))
        decay = jnp.exp2(old - top)
        weights = jnp.exp2(s - top)
        l_s[:, cols] = l_s[:, cols] * decay + jnp.sum(weights, axis=0, keepdims=True)
        m_s[:, cols] = top
        part = lax.dot_general(
            values,
            weights.astype(jnp.bfloat16),
            (((0,), (0,)), ((), ())),
            preferred_element_type=jnp.float32,
        )
        acc[:, cols] = acc[:, cols] * decay + part

    def comp_block(n):
        return (lambda: cbuf[n, 0]), (lambda: cbuf[n, 1]), n

    def prompt_block(j, count, slot, slots):
        def read(kv):
            return pbuf[j : j + count, slot : slot + slots, kv].reshape(4 * HALF, HD)

        return (lambda: read(0)), (lambda: read(1)), None

    def attend(block, later_block):
        keys, values, distance = block
        second = first_scores(keys(), 1)
        softmax_part(sb[...], 0, values(), distance)
        if later_block is not None:
            sb[...] = first_scores(later_block[0](), 0)
        softmax_part(second, 1, values(), distance)

    sb[...] = first_scores(cbuf[0, 0], 0)
    attend(comp_block(0), None)

    spot = c % PER_GROUP
    pl.semaphore_wait(barrier, 11 - spot // 15 - spot // 14)

    def remote(src, dst, send, recv, device):
        return pltpu.make_async_remote_copy(
            src_ref=src, dst_ref=dst, send_sem=send, recv_sem=recv, device_id=device, device_id_type=MESH
        )

    later = [
        remote(cbuf.at[0, co], cbuf.at[n, co], up_send.at[n], up_recv.at[n], (p, c + n)) for n in (1, 2)
    ]
    for n in (1, 2):
        pl.when(spot < 16 - n)(later[n - 1].start)

    prompt_id = group_prompt[group]
    direct = []
    for j in list(range(1, N_MSG + 1)) + list(range(N_MSG + 2, N_LOAD)):
        second = j // (N_MSG + 1)
        m, n = (j, j - 1) if j <= N_MSG else (j - (N_MSG + 1) + FAR, j - 2)
        loads[j].wait()
        for kv in range(2):
            sbuf[n, kv] = stage[j][kv, prompt_id]
        if second:
            copy = remote(sbuf.at[n], pbuf.at[m, 2], par_send.at[m], par_recv.at[m], at(*MOVES[m - 1]))
        else:
            copy = remote(sbuf.at[n], pbuf.at[m, 0], dir_send.at[m], dir_recv.at[m], at(*MOVES[m - 1]))
        copy.start()
        direct.append(copy)
    for j, slot in ((0, 0), (N_MSG + 1, 1)):
        loads[j].wait()
        for kv in range(2):
            pbuf[0, slot, kv] = stage[j][kv, prompt_id]
    own_pair = remote(
        pbuf.at[0, pl.ds(0, 2)], pbuf.at[0, pl.ds(2, 2)], sib_send.at[0, 0], sib_recv.at[0, 0], sibling
    )
    own_pair.start()

    def to_partner(j):
        return remote(pbuf.at[j, 0], pbuf.at[j, 2], par_send.at[j], par_recv.at[j], partner)

    def to_sibling(j, slot):
        return remote(
            pbuf.at[j, slot],
            pbuf.at[j, slot + 1],
            sib_send.at[j, slot // 2],
            sib_recv.at[j, slot // 2],
            sibling,
        )

    def serve_direct(j):
        remote(sbuf.at[j - 1], pbuf.at[j, 0], dir_send.at[j], dir_recv.at[j], sibling).wait_recv()
        if j <= FAR:
            to_partner(j).start()
        to_sibling(j, 0).start()

    def serve_partner(j):
        to_partner(j).wait_recv()
        to_sibling(j, 2).start()

    earlier = {
        n: remote(cbuf.at[n, co], cbuf.at[n, co], sibc_send.at[n - 1], sibc_recv.at[n - 1], sibling)
        for n in (1, 2)
    }

    def serve_comp(n):
        pl.when(spot >= n)(later[n - 1].wait_recv)

        @pl.when(spot < n)
        def _():
            cbuf[n, co] = jnp.zeros((ROWS, HD), jnp.bfloat16)

        earlier[n].start()

    serve = {"D": serve_direct, "P": serve_partner, "C": serve_comp}

    def ready(name):
        for kind, j in NEEDS[name]:
            if kind == "O":
                own_pair.wait_recv()
            elif kind == "C":
                earlier[j].wait_recv()
            else:
                to_sibling(j, 0 if kind == "D" else 2).wait_recv()

    blocks = {
        "O": prompt_block(0, 1, 0, 4),
        "D1": prompt_block(1, 2, 0, 2),
        "D3": prompt_block(3, 2, 0, 2),
        "P1": prompt_block(1, 2, 2, 2),
        "P3": prompt_block(3, 2, 2, 2),
        "D5": prompt_block(5, 2, 0, 2),
        "P5": prompt_block(5, 2, 2, 2),
        "N5": prompt_block(5, 1, 0, 4),
        "N6": prompt_block(6, 1, 0, 4),
        "N7": prompt_block(7, 1, 0, 4),
        "C1": comp_block(1),
        "C2": comp_block(2),
    }
    for n, name in enumerate(ORDER):
        for kind, j in SERVE[n]:
            serve[kind](j)
        if n == 0 or ORDER[n - 1] not in AHEAD:
            ready(name)
            sb[...] = first_scores(blocks[name][0](), 0)
        following = None
        if name in AHEAD:
            following = ORDER[n + 1]
            ready(following)
        attend(blocks[name], blocks.get(following))

    for n in range(HERE):
        cols = slice(n * ROWS, (n + 1) * ROWS)
        out = acc[:, cols] / l_s[:, cols]
        out_ref[:, n * HD : (n + 1) * HD] = out.T.astype(jnp.bfloat16)

    for n in (1, 2):
        pl.when(spot < 16 - n)(later[n - 1].wait_send)
    for n in (1, 2):
        earlier[n].wait_send()
    own_pair.wait_send()
    for copy in direct:
        copy.wait_send()

    for j in range(1, N_MSG + 1):
        if j <= FAR:
            to_partner(j).wait_send()
        to_sibling(j, 0).wait_send()
        to_sibling(j, 2).wait_send()


def body(queries, comp_kv, prompt_kv, comp_lengths, group_prompt):
    bf16 = jnp.bfloat16
    dma = pltpu.SemaphoreType.DMA
    return pl.pallas_call(
        kernel,
        out_shape=jax.ShapeDtypeStruct((ROWS, HERE * HD), bf16),
        in_specs=[pl.BlockSpec(memory_space=pltpu.HBM)] * 5,
        out_specs=pl.BlockSpec(memory_space=pltpu.VMEM),
        scratch_shapes=[
            pltpu.SMEM((2, PER_GROUP), jnp.int32),
            pltpu.SMEM((2,), jnp.int32),
            pltpu.VMEM((ROWS, ROWS), jnp.float32),
            pltpu.VMEM((ROWS, HERE * HD), bf16),
            *[pltpu.VMEM((2, 8, HALF, HD), bf16) for _ in range(N_LOAD)],
            pltpu.VMEM((2 * N_MSG - FAR, 2, HALF, HD), bf16),
            pltpu.VMEM((3, 2, ROWS, HD), bf16),
            pltpu.VMEM((N_MSG + 1, 4, 2, HALF, HD), bf16),
            pltpu.VMEM((2 * HD, HERE * ROWS), bf16),
            pltpu.VMEM((HD, HERE * ROWS), jnp.float32),
            pltpu.VMEM((1, HERE * ROWS), jnp.float32),
            pltpu.VMEM((1, HERE * ROWS), jnp.float32),
            dma((2,)),
            dma(()),
            dma(()),
            dma((N_LOAD,)),
            dma((3,)),
            dma((3,)),
            dma((2,)),
            dma((2,)),
            dma((N_MSG + 1,)),
            dma((N_MSG + 1,)),
            dma((N_MSG + 1,)),
            dma((N_MSG + 1,)),
            dma((N_MSG + 1, 2)),
            dma((N_MSG + 1, 2)),
        ],
        compiler_params=pltpu.CompilerParams(
            collective_id=0, has_side_effects=True, vmem_limit_bytes=48 * 2**20
        ),
        cost_estimate=pl.CostEstimate(
            flops=4 * 1024 * 5632 * HD, bytes_accessed=12 * 2**20, transcendentals=1024 * 5632
        ),
    )(*[pltpu.with_memory_space_constraint(a, pltpu.HBM) for a in (queries, comp_kv, prompt_kv, comp_lengths, group_prompt)])


def solution(mesh):
    placed = (P("comp", "prompt"), P(None, "comp", None), P(None, None, "prompt", None), P(), P())
    return jax.shard_map(
        body, mesh=mesh, in_specs=placed, out_specs=P("comp", "prompt"), check_vma=False
    )
```

```python
import functools
import math

import jax
import jax.numpy as jnp
from jax import lax
from jax.experimental import pallas as pl
from jax.experimental.pallas import tpu as pltpu
from jax.sharding import PartitionSpec as P

HEADS = 32
KV_HEADS = 8
HD = 128
ROWS = 512
TOK = 256
HALF = 128
HERE = 2
PER_GROUP = 16
SCALE = math.log2(math.e) / math.sqrt(HD)
MESH = pl.DeviceIdType.MESH
MOVES = ((1, 0), (3, 0), (0, 1), (1, 1), (3, 1), (2, 0), (2, 1))
N_MSG = len(MOVES)
FAR = 7
N_LOAD = N_MSG + 2 + N_MSG - FAR
ORDER = ("O", "D1", "C2", "D3", "C1", "D5", "P1", "P3", "P5", "N7")
AHEAD = ("O", "D1", "C2", "D3", "C1", "D5", "P1", "P3", "P5",)
SERVE = (
    (("D", 1), ("D", 2), ("C", 2),),
    (("D", 3), ("D", 4),),
    (("D", 5), ("C", 1),),
    (("D", 6), ("D", 7),),
    (("P", 1), ("P", 2),),
    (("P", 3), ("P", 4),),
    (("P", 5), ("P", 6),),
    (("P", 7),),
    (),
    (),
)
NEEDS = {
    "O": (("O", 0),),
    "D1": (("D", 1), ("D", 2)),
    "D3": (("D", 3), ("D", 4)),
    "P1": (("P", 1), ("P", 2)),
    "P3": (("P", 3), ("P", 4)),
    "D5": (("D", 5), ("D", 6)),
    "P5": (("P", 5), ("P", 6)),
    "N5": (("D", 5), ("P", 5)),
    "N6": (("D", 6), ("P", 6)),
    "N7": (("D", 7), ("P", 7)),
    "C1": (("C", 1),),
    "C2": (("C", 2),),
}


def kernel(
    q_hbm, comp_hbm, prompt_hbm, lengths_hbm, group_prompt_hbm, out_ref,
    lengths, group_prompt, sb, q_buf, stage_0, stage_1, stage_2, stage_3, stage_4, stage_5, stage_6, stage_7, stage_8, sbuf, cbuf, pbuf, qt, acc, m_s, l_s,
    small_sem, q_sem, own_sem, stage_sem,
    up_send, up_recv, sibc_send, sibc_recv,
    dir_send, dir_recv, par_send, par_recv, sib_send, sib_recv,
):
    p, c = lax.axis_index("prompt"), lax.axis_index("comp")
    x, h, co = p // 4, (p // 2) % 2, p % 2
    z, lo = c // 2, c % 2
    group = c // PER_GROUP
    head = p // 2
    sibling = (p + 1 - 2 * co, c)
    partner = (p, c + (1 - co) * (1 - 2 * lo) + co * (2 - 4 * (z % 2)))

    def at(dx, dh):
        return ((x + dx + 4) % 4) * 4 + ((h + dh) % 2) * 2 + co, z * 2 + (lo + dh) % 2

    stage = [stage_0, stage_1, stage_2, stage_3, stage_4, stage_5, stage_6, stage_7, stage_8]

    small = [
        pltpu.make_async_copy(lengths_hbm, lengths, small_sem.at[0]),
        pltpu.make_async_copy(group_prompt_hbm, group_prompt, small_sem.at[1]),
    ]
    for copy in small:
        copy.start()
    q_copy = pltpu.make_async_copy(q_hbm, q_buf, q_sem)
    q_copy.start()
    own_copy = pltpu.make_async_copy(
        comp_hbm.at[:, :, pl.ds(pl.multiple_of(head * HD, HD), HD)], cbuf.at[0], own_sem
    )
    own_copy.start()
    loads = []
    for j in range(N_LOAD):
        if j in (0, N_MSG + 1):
            to_head, half = head, j // (N_MSG + 1)
        else:
            second = j // (N_MSG + 1)
            dx, dh = MOVES[j - 1 if j <= N_MSG else j - (N_MSG + 2) + FAR]
            to_head = at(dx, dh)[0] // 2
            half = (z + (lo + dh) % 2 + second) % 2
        copy = pltpu.make_async_copy(
            prompt_hbm.at[
                :,
                :,
                pl.ds(pl.multiple_of(half * HALF, HALF), HALF),
                pl.ds(pl.multiple_of(to_head * HD, HD), HD),
            ],
            stage[j],
            stage_sem.at[j],
        )
        loads.append(copy)
    for j in list(range(1, N_MSG + 1)) + list(range(N_MSG + 2, N_LOAD)) + [0, N_MSG + 1]:
        loads[j].start()

    barrier = pltpu.get_barrier_semaphore()

    def tell(device):
        pl.semaphore_signal(barrier, inc=1, device_id=device, device_id_type=MESH)

    for dx, dh in MOVES:
        tell(at(-dx, dh))
    tell(sibling)
    tell(partner)
    for n in (1, 2):

        @pl.when(c % PER_GROUP >= n)
        def _():
            tell((p, c - n))

    q_copy.wait()
    for n in range(HERE):
        q = q_buf[:, n * HD : (n + 1) * HD].astype(jnp.float32) * SCALE
        q = q.T
        high = q.astype(jnp.bfloat16)
        qt[0:HD, n * ROWS : (n + 1) * ROWS] = high
        qt[HD : 2 * HD, n * ROWS : (n + 1) * ROWS] = (q - high.astype(jnp.float32)).astype(
            jnp.bfloat16
        )
    m_s[...] = jnp.full_like(m_s, -1e30)
    l_s[...] = jnp.zeros_like(l_s)
    acc[...] = jnp.zeros_like(acc)

    own_copy.wait()
    for copy in small:
        copy.wait()

    lane = lax.broadcasted_iota(jnp.int32, (1, ROWS), 1)
    base = (c % PER_GROUP) * ROWS
    offset = lane + base
    first = jnp.zeros_like(offset)
    end = jnp.int32(0)
    for n in range(lengths.shape[1]):
        end = end + lengths[group, n]
        first = jnp.where(offset >= end, end, first)
    first = first - base

    def first_scores(keys, n):
        return jnp.dot(
            jnp.concatenate([keys, keys], axis=1),
            qt[:, n * ROWS : (n + 1) * ROWS],
            preferred_element_type=jnp.float32,
        )

    def softmax_part(s, n, values, distance):
        cols = slice(n * ROWS, (n + 1) * ROWS)
        if distance is not None:
            key = lax.broadcasted_iota(jnp.int32, (ROWS, ROWS), 0)
            seen = key >= first + distance * ROWS
            if distance == 0:
                seen = seen & (key <= lane)
            s = jnp.where(seen, s, -1e30)
        old = m_s[:, cols]
        top = jnp.maximum(old, jnp.max(s, axis=0, keepdims=True))
        decay = jnp.exp2(old - top)
        weights = jnp.exp2(s - top)
        l_s[:, cols] = l_s[:, cols] * decay + jnp.sum(weights, axis=0, keepdims=True)
        m_s[:, cols] = top
        part = lax.dot_general(
            values,
            weights.astype(jnp.bfloat16),
            (((0,), (0,)), ((), ())),
            preferred_element_type=jnp.float32,
        )
        acc[:, cols] = acc[:, cols] * decay + part

    def comp_block(n):
        return (lambda: cbuf[n, 0]), (lambda: cbuf[n, 1]), n

    def prompt_block(j, count, slot, slots):
        def read(kv):
            return pbuf[j : j + count, slot : slot + slots, kv].reshape(4 * HALF, HD)

        return (lambda: read(0)), (lambda: read(1)), None

    def attend(block, later_block):
        keys, values, distance = block
        second = first_scores(keys(), 1)
        softmax_part(sb[...], 0, values(), distance)
        if later_block is not None:
            sb[...] = first_scores(later_block[0](), 0)
        softmax_part(second, 1, values(), distance)

    sb[...] = first_scores(cbuf[0, 0], 0)
    attend(comp_block(0), None)

    spot = c % PER_GROUP
    pl.semaphore_wait(barrier, 11 - spot // 15 - spot // 14)

    def remote(src, dst, send, recv, device):
        return pltpu.make_async_remote_copy(
            src_ref=src, dst_ref=dst, send_sem=send, recv_sem=recv, device_id=device, device_id_type=MESH
        )

    later = [
        remote(cbuf.at[0, co], cbuf.at[n, co], up_send.at[n], up_recv.at[n], (p, c + n)) for n in (1, 2)
    ]
    for n in (1, 2):
        pl.when(spot < 16 - n)(later[n - 1].start)

    prompt_id = group_prompt[group]
    direct = []
    for j in list(range(1, N_MSG + 1)) + list(range(N_MSG + 2, N_LOAD)):
        second = j // (N_MSG + 1)
        m, n = (j, j - 1) if j <= N_MSG else (j - (N_MSG + 1) + FAR, j - 2)
        loads[j].wait()
        for kv in range(2):
            sbuf[n, kv] = stage[j][kv, prompt_id]
        if second:
            copy = remote(sbuf.at[n], pbuf.at[m, 2], par_send.at[m], par_recv.at[m], at(*MOVES[m - 1]))
        else:
            copy = remote(sbuf.at[n], pbuf.at[m, 0], dir_send.at[m], dir_recv.at[m], at(*MOVES[m - 1]))
        copy.start()
        direct.append(copy)
    for j, slot in ((0, 0), (N_MSG + 1, 1)):
        loads[j].wait()
        for kv in range(2):
            pbuf[0, slot, kv] = stage[j][kv, prompt_id]
    own_pair = remote(
        pbuf.at[0, pl.ds(0, 2)], pbuf.at[0, pl.ds(2, 2)], sib_send.at[0, 0], sib_recv.at[0, 0], sibling
    )
    own_pair.start()

    def to_partner(j):
        return remote(pbuf.at[j, 0], pbuf.at[j, 2], par_send.at[j], par_recv.at[j], partner)

    def to_sibling(j, slot):
        return remote(
            pbuf.at[j, slot],
            pbuf.at[j, slot + 1],
            sib_send.at[j, slot // 2],
            sib_recv.at[j, slot // 2],
            sibling,
        )

    def serve_direct(j):
        remote(sbuf.at[j - 1], pbuf.at[j, 0], dir_send.at[j], dir_recv.at[j], sibling).wait_recv()
        if j <= FAR:
            to_partner(j).start()
        to_sibling(j, 0).start()

    def serve_partner(j):
        to_partner(j).wait_recv()
        to_sibling(j, 2).start()

    earlier = {
        n: remote(cbuf.at[n, co], cbuf.at[n, co], sibc_send.at[n - 1], sibc_recv.at[n - 1], sibling)
        for n in (1, 2)
    }

    def serve_comp(n):
        pl.when(spot >= n)(later[n - 1].wait_recv)

        @pl.when(spot < n)
        def _():
            cbuf[n, co] = jnp.zeros((ROWS, HD), jnp.bfloat16)

        earlier[n].start()

    serve = {"D": serve_direct, "P": serve_partner, "C": serve_comp}

    def ready(name):
        for kind, j in NEEDS[name]:
            if kind == "O":
                own_pair.wait_recv()
            elif kind == "C":
                earlier[j].wait_recv()
            else:
                to_sibling(j, 0 if kind == "D" else 2).wait_recv()

    blocks = {
        "O": prompt_block(0, 1, 0, 4),
        "D1": prompt_block(1, 2, 0, 2),
        "D3": prompt_block(3, 2, 0, 2),
        "P1": prompt_block(1, 2, 2, 2),
        "P3": prompt_block(3, 2, 2, 2),
        "D5": prompt_block(5, 2, 0, 2),
        "P5": prompt_block(5, 2, 2, 2),
        "N5": prompt_block(5, 1, 0, 4),
        "N6": prompt_block(6, 1, 0, 4),
        "N7": prompt_block(7, 1, 0, 4),
        "C1": comp_block(1),
        "C2": comp_block(2),
    }
    for n, name in enumerate(ORDER):
        for kind, j in SERVE[n]:
            serve[kind](j)
        if n == 0 or ORDER[n - 1] not in AHEAD:
            ready(name)
            sb[...] = first_scores(blocks[name][0](), 0)
        following = None
        if name in AHEAD:
            following = ORDER[n + 1]
            ready(following)
        attend(blocks[name], blocks.get(following))

    for n in range(HERE):
        cols = slice(n * ROWS, (n + 1) * ROWS)
        out = acc[:, cols] / l_s[:, cols]
        out_ref[:, n * HD : (n + 1) * HD] = out.T.astype(jnp.bfloat16)

    for n in (1, 2):
        pl.when(spot < 16 - n)(later[n - 1].wait_send)
    for n in (1, 2):
        earlier[n].wait_send()
    own_pair.wait_send()
    for copy in direct:
        copy.wait_send()

    for j in range(1, N_MSG + 1):
        if j <= FAR:
            to_partner(j).wait_send()
        to_sibling(j, 0).wait_send()
        to_sibling(j, 2).wait_send()


def body(queries, comp_kv, prompt_kv, comp_lengths, group_prompt):
    bf16 = jnp.bfloat16
    dma = pltpu.SemaphoreType.DMA
    return pl.pallas_call(
        kernel,
        out_shape=jax.ShapeDtypeStruct((ROWS, HERE * HD), bf16),
        in_specs=[pl.BlockSpec(memory_space=pltpu.HBM)] * 5,
        out_specs=pl.BlockSpec(memory_space=pltpu.VMEM),
        scratch_shapes=[
            pltpu.SMEM((2, PER_GROUP), jnp.int32),
            pltpu.SMEM((2,), jnp.int32),
            pltpu.VMEM((ROWS, ROWS), jnp.float32),
            pltpu.VMEM((ROWS, HERE * HD), bf16),
            *[pltpu.VMEM((2, 8, HALF, HD), bf16) for _ in range(N_LOAD)],
            pltpu.VMEM((2 * N_MSG - FAR, 2, HALF, HD), bf16),
            pltpu.VMEM((3, 2, ROWS, HD), bf16),
            pltpu.VMEM((N_MSG + 1, 4, 2, HALF, HD), bf16),
            pltpu.VMEM((2 * HD, HERE * ROWS), bf16),
            pltpu.VMEM((HD, HERE * ROWS), jnp.float32),
            pltpu.VMEM((1, HERE * ROWS), jnp.float32),
            pltpu.VMEM((1, HERE * ROWS), jnp.float32),
            dma((2,)),
            dma(()),
            dma(()),
            dma((N_LOAD,)),
            dma((3,)),
            dma((3,)),
            dma((2,)),
            dma((2,)),
            dma((N_MSG + 1,)),
            dma((N_MSG + 1,)),
            dma((N_MSG + 1,)),
            dma((N_MSG + 1,)),
            dma((N_MSG + 1, 2)),
            dma((N_MSG + 1, 2)),
        ],
        compiler_params=pltpu.CompilerParams(
            collective_id=0, has_side_effects=True, vmem_limit_bytes=48 * 2**20
        ),
        cost_estimate=pl.CostEstimate(
            flops=4 * 1024 * 5632 * HD, bytes_accessed=12 * 2**20, transcendentals=1024 * 5632
        ),
    )(*[pltpu.with_memory_space_constraint(a, pltpu.HBM) for a in (queries, comp_kv, prompt_kv, comp_lengths, group_prompt)])


def solution(mesh):
    placed = (P("comp", "prompt"), P(None, "comp", None), P(None, None, "prompt", None), P(), P())
    return jax.shard_map(
        body, mesh=mesh, in_specs=placed, out_specs=P("comp", "prompt"), check_vma=False
    )
```

```python
import functools
import math

import jax
import jax.numpy as jnp
from jax import lax
from jax.experimental import pallas as pl
from jax.experimental.pallas import tpu as pltpu
from jax.sharding import PartitionSpec as P

HEADS = 32
KV_HEADS = 8
HD = 128
ROWS = 512
TOK = 256
HALF = 128
HERE = 2
PER_GROUP = 16
N_COMP = 32
SCALE = math.log2(math.e) / math.sqrt(HD)
MESH = pl.DeviceIdType.MESH
MOVES = ((3, 0), (1, 0), (0, 1), (3, 1), (1, 1), (2, 0), (2, 1))
N_MSG = len(MOVES)
FAR = 7
N_LOAD = N_MSG + 2 + N_MSG - FAR
ORDER = ("O", "D1", "C2", "D3", "C1", "D5", "P1", "P3", "P5", "N7")
AHEAD = ("O", "D1", "C2", "D3", "C1", "D5", "P1", "P3", "P5",)
SERVE = (
    (("D", 1), ("D", 2), ("C", 2),),
    (("D", 3), ("D", 4),),
    (("D", 5), ("C", 1),),
    (("D", 6), ("D", 7),),
    (("P", 1), ("P", 2),),
    (("P", 3), ("P", 4),),
    (("P", 5), ("P", 6),),
    (("P", 7),),
    (),
    (),
)
NEEDS = {
    "O": (("O", 0),),
    "D1": (("D", 1), ("D", 2)),
    "D3": (("D", 3), ("D", 4)),
    "P1": (("P", 1), ("P", 2)),
    "P3": (("P", 3), ("P", 4)),
    "D5": (("D", 5), ("D", 6)),
    "P5": (("P", 5), ("P", 6)),
    "N5": (("D", 5), ("P", 5)),
    "N6": (("D", 6), ("P", 6)),
    "N7": (("D", 7), ("P", 7)),
    "C1": (("C", 1),),
    "C2": (("C", 2),),
}


def kernel(
    q_hbm, comp_hbm, prompt_hbm, lengths_hbm, group_prompt_hbm, out_ref,
    lengths, group_prompt, sb, q_buf, stage_0, stage_1, stage_2, stage_3, stage_4, stage_5, stage_6, stage_7, stage_8, sbuf, cbuf, pbuf, qt, acc, m_s, l_s,
    small_sem, q_sem, own_sem, stage_sem,
    up_send, up_recv, sibc_send, sibc_recv,
    dir_send, dir_recv, par_send, par_recv, sib_send, sib_recv,
):
    p, c = lax.axis_index("prompt"), lax.axis_index("comp")
    x, h, co = p // 4, (p // 2) % 2, p % 2
    z, lo = c // 2, c % 2
    group = c // PER_GROUP
    head = p // 2
    sibling = (p + 1 - 2 * co, c)
    partner = (p, c + (1 - co) * (1 - 2 * lo) + co * (2 - 4 * (z % 2)))

    def at(dx, dh):
        return ((x + dx + 4) % 4) * 4 + ((h + dh) % 2) * 2 + co, z * 2 + (lo + dh) % 2

    stage = [stage_0, stage_1, stage_2, stage_3, stage_4, stage_5, stage_6, stage_7, stage_8]

    small = [
        pltpu.make_async_copy(lengths_hbm, lengths, small_sem.at[0]),
        pltpu.make_async_copy(group_prompt_hbm, group_prompt, small_sem.at[1]),
    ]
    for copy in small:
        copy.start()
    q_copy = pltpu.make_async_copy(q_hbm, q_buf, q_sem)
    q_copy.start()
    own_copy = pltpu.make_async_copy(
        comp_hbm.at[:, :, pl.ds(pl.multiple_of(head * HD, HD), HD)], cbuf.at[0], own_sem
    )
    own_copy.start()
    loads = []
    for j in range(N_LOAD):
        if j in (0, N_MSG + 1):
            to_head, half = head, j // (N_MSG + 1)
        else:
            second = j // (N_MSG + 1)
            dx, dh = MOVES[j - 1 if j <= N_MSG else j - (N_MSG + 2) + FAR]
            to_head = at(dx, dh)[0] // 2
            half = (z + (lo + dh) % 2 + second) % 2
        copy = pltpu.make_async_copy(
            prompt_hbm.at[
                :,
                :,
                pl.ds(pl.multiple_of(half * HALF, HALF), HALF),
                pl.ds(pl.multiple_of(to_head * HD, HD), HD),
            ],
            stage[j],
            stage_sem.at[j],
        )
        loads.append(copy)
    for j in list(range(1, N_MSG + 1)) + list(range(N_MSG + 2, N_LOAD)) + [0, N_MSG + 1]:
        loads[j].start()

    barrier = pltpu.get_barrier_semaphore()

    def tell(device):
        pl.semaphore_signal(barrier, inc=1, device_id=device, device_id_type=MESH)

    for dx, dh in MOVES:
        tell(at(-dx, dh))
    tell(sibling)
    tell(partner)
    for n in (1, 2):

        @pl.when(c % PER_GROUP >= n)
        def _():
            tell((p, c - n))

    q_copy.wait()
    for n in range(HERE):
        q = q_buf[:, n * HD : (n + 1) * HD].astype(jnp.float32) * SCALE
        q = q.T
        high = q.astype(jnp.bfloat16)
        qt[0:HD, n * ROWS : (n + 1) * ROWS] = high
        qt[HD : 2 * HD, n * ROWS : (n + 1) * ROWS] = (q - high.astype(jnp.float32)).astype(
            jnp.bfloat16
        )
    m_s[...] = jnp.full_like(m_s, -1e30)
    l_s[...] = jnp.zeros_like(l_s)
    acc[...] = jnp.zeros_like(acc)

    own_copy.wait()
    for copy in small:
        copy.wait()

    lane = lax.broadcasted_iota(jnp.int32, (1, ROWS), 1)
    base = (c % PER_GROUP) * ROWS
    offset = lane + base
    first = jnp.zeros_like(offset)
    end = jnp.int32(0)
    for n in range(lengths.shape[1]):
        end = end + lengths[group, n]
        first = jnp.where(offset >= end, end, first)
    first = first - base

    def first_scores(keys, n):
        return jnp.dot(
            jnp.concatenate([keys, keys], axis=1),
            qt[:, n * ROWS : (n + 1) * ROWS],
            preferred_element_type=jnp.float32,
        )

    def softmax_part(s, n, values, distance):
        cols = slice(n * ROWS, (n + 1) * ROWS)
        if distance is not None:
            key = lax.broadcasted_iota(jnp.int32, (ROWS, ROWS), 0)
            seen = key >= first + distance * ROWS
            if distance == 0:
                seen = seen & (key <= lane)
            s = jnp.where(seen, s, -1e30)
        old = m_s[:, cols]
        top = jnp.maximum(old, jnp.max(s, axis=0, keepdims=True))
        decay = jnp.exp2(old - top)
        weights = jnp.exp2(s - top)
        l_s[:, cols] = l_s[:, cols] * decay + jnp.sum(weights, axis=0, keepdims=True)
        m_s[:, cols] = top
        part = lax.dot_general(
            values,
            weights.astype(jnp.bfloat16),
            (((0,), (0,)), ((), ())),
            preferred_element_type=jnp.float32,
        )
        acc[:, cols] = acc[:, cols] * decay + part

    def comp_block(n):
        return (lambda: cbuf[n, 0]), (lambda: cbuf[n, 1]), n

    def prompt_block(j, count, slot, slots):
        def read(kv):
            return pbuf[j : j + count, slot : slot + slots, kv].reshape(4 * HALF, HD)

        return (lambda: read(0)), (lambda: read(1)), None

    def attend(block, later_block):
        keys, values, distance = block
        second = first_scores(keys(), 1)
        softmax_part(sb[...], 0, values(), distance)
        if later_block is not None:
            sb[...] = first_scores(later_block[0](), 0)
        softmax_part(second, 1, values(), distance)

    sb[...] = first_scores(cbuf[0, 0], 0)
    attend(comp_block(0), None)

    spot = c % PER_GROUP
    pl.semaphore_wait(barrier, 11 - spot // 15 - spot // 14)

    def remote(src, dst, send, recv, device):
        return pltpu.make_async_remote_copy(
            src_ref=src, dst_ref=dst, send_sem=send, recv_sem=recv, device_id=device, device_id_type=MESH
        )

    later = [
        remote(cbuf.at[0, co], cbuf.at[n, co], up_send.at[n], up_recv.at[n], (p, (c + n) % N_COMP)) for n in (1, 2)
    ]
    for n in (1, 2):
        pl.when(spot < 16 - n)(later[n - 1].start)

    prompt_id = group_prompt[group]
    direct = []
    for j in list(range(1, N_MSG + 1)) + list(range(N_MSG + 2, N_LOAD)):
        second = j // (N_MSG + 1)
        m, n = (j, j - 1) if j <= N_MSG else (j - (N_MSG + 1) + FAR, j - 2)
        loads[j].wait()
        for kv in range(2):
            sbuf[n, kv] = stage[j][kv, prompt_id]
        if second:
            copy = remote(sbuf.at[n], pbuf.at[m, 2], par_send.at[m], par_recv.at[m], at(*MOVES[m - 1]))
        else:
            copy = remote(sbuf.at[n], pbuf.at[m, 0], dir_send.at[m], dir_recv.at[m], at(*MOVES[m - 1]))
        copy.start()
        direct.append(copy)
    for j, slot in ((0, 0), (N_MSG + 1, 1)):
        loads[j].wait()
        for kv in range(2):
            pbuf[0, slot, kv] = stage[j][kv, prompt_id]
    own_pair = remote(
        pbuf.at[0, pl.ds(0, 2)], pbuf.at[0, pl.ds(2, 2)], sib_send.at[0, 0], sib_recv.at[0, 0], sibling
    )
    own_pair.start()

    def to_partner(j):
        return remote(pbuf.at[j, 0], pbuf.at[j, 2], par_send.at[j], par_recv.at[j], partner)

    def to_sibling(j, slot):
        return remote(
            pbuf.at[j, slot],
            pbuf.at[j, slot + 1],
            sib_send.at[j, slot // 2],
            sib_recv.at[j, slot // 2],
            sibling,
        )

    def serve_direct(j):
        remote(sbuf.at[j - 1], pbuf.at[j, 0], dir_send.at[j], dir_recv.at[j], sibling).wait_recv()
        if j <= FAR:
            to_partner(j).start()
        to_sibling(j, 0).start()

    def serve_partner(j):
        to_partner(j).wait_recv()
        to_sibling(j, 2).start()

    earlier = {
        n: remote(cbuf.at[n, co], cbuf.at[n, co], sibc_send.at[n - 1], sibc_recv.at[n - 1], sibling)
        for n in (1, 2)
    }

    def serve_comp(n):
        pl.when(spot >= n)(later[n - 1].wait_recv)

        @pl.when(spot < n)
        def _():
            cbuf[n, co] = jnp.zeros((ROWS, HD), jnp.bfloat16)

        earlier[n].start()

    serve = {"D": serve_direct, "P": serve_partner, "C": serve_comp}

    def ready(name):
        for kind, j in NEEDS[name]:
            if kind == "O":
                own_pair.wait_recv()
            elif kind == "C":
                earlier[j].wait_recv()
            else:
                to_sibling(j, 0 if kind == "D" else 2).wait_recv()

    blocks = {
        "O": prompt_block(0, 1, 0, 4),
        "D1": prompt_block(1, 2, 0, 2),
        "D3": prompt_block(3, 2, 0, 2),
        "P1": prompt_block(1, 2, 2, 2),
        "P3": prompt_block(3, 2, 2, 2),
        "D5": prompt_block(5, 2, 0, 2),
        "P5": prompt_block(5, 2, 2, 2),
        "N5": prompt_block(5, 1, 0, 4),
        "N6": prompt_block(6, 1, 0, 4),
        "N7": prompt_block(7, 1, 0, 4),
        "C1": comp_block(1),
        "C2": comp_block(2),
    }
    for n, name in enumerate(ORDER):
        for kind, j in SERVE[n]:
            serve[kind](j)
        if n == 0 or ORDER[n - 1] not in AHEAD:
            ready(name)
            sb[...] = first_scores(blocks[name][0](), 0)
        following = None
        if name in AHEAD:
            following = ORDER[n + 1]
            ready(following)
        attend(blocks[name], blocks.get(following))

    for n in range(HERE):
        cols = slice(n * ROWS, (n + 1) * ROWS)
        out = acc[:, cols] / l_s[:, cols]
        out_ref[:, n * HD : (n + 1) * HD] = out.T.astype(jnp.bfloat16)

    for n in (1, 2):
        pl.when(spot < 16 - n)(later[n - 1].wait_send)
    for n in (1, 2):
        earlier[n].wait_send()
    own_pair.wait_send()
    for copy in direct:
        copy.wait_send()

    for j in range(1, N_MSG + 1):
        if j <= FAR:
            to_partner(j).wait_send()
        to_sibling(j, 0).wait_send()
        to_sibling(j, 2).wait_send()


def body(queries, comp_kv, prompt_kv, comp_lengths, group_prompt):
    bf16 = jnp.bfloat16
    dma = pltpu.SemaphoreType.DMA
    return pl.pallas_call(
        kernel,
        out_shape=jax.ShapeDtypeStruct((ROWS, HERE * HD), bf16),
        in_specs=[pl.BlockSpec(memory_space=pltpu.HBM)] * 5,
        out_specs=pl.BlockSpec(memory_space=pltpu.VMEM),
        scratch_shapes=[
            pltpu.SMEM((2, PER_GROUP), jnp.int32),
            pltpu.SMEM((2,), jnp.int32),
            pltpu.VMEM((ROWS, ROWS), jnp.float32),
            pltpu.VMEM((ROWS, HERE * HD), bf16),
            *[pltpu.VMEM((2, 8, HALF, HD), bf16) for _ in range(N_LOAD)],
            pltpu.VMEM((2 * N_MSG - FAR, 2, HALF, HD), bf16),
            pltpu.VMEM((3, 2, ROWS, HD), bf16),
            pltpu.VMEM((N_MSG + 1, 4, 2, HALF, HD), bf16),
            pltpu.VMEM((2 * HD, HERE * ROWS), bf16),
            pltpu.VMEM((HD, HERE * ROWS), jnp.float32),
            pltpu.VMEM((1, HERE * ROWS), jnp.float32),
            pltpu.VMEM((1, HERE * ROWS), jnp.float32),
            dma((2,)),
            dma(()),
            dma(()),
            dma((N_LOAD,)),
            dma((3,)),
            dma((3,)),
            dma((2,)),
            dma((2,)),
            dma((N_MSG + 1,)),
            dma((N_MSG + 1,)),
            dma((N_MSG + 1,)),
            dma((N_MSG + 1,)),
            dma((N_MSG + 1, 2)),
            dma((N_MSG + 1, 2)),
        ],
        compiler_params=pltpu.CompilerParams(
            collective_id=0, has_side_effects=True, vmem_limit_bytes=48 * 2**20
        ),
        cost_estimate=pl.CostEstimate(
            flops=4 * 1024 * 5632 * HD, bytes_accessed=12 * 2**20, transcendentals=1024 * 5632
        ),
    )(*[pltpu.with_memory_space_constraint(a, pltpu.HBM) for a in (queries, comp_kv, prompt_kv, comp_lengths, group_prompt)])


def solution(mesh):
    placed = (P("comp", "prompt"), P(None, "comp", None), P(None, None, "prompt", None), P(), P())
    return jax.shard_map(
        body, mesh=mesh, in_specs=placed, out_specs=P("comp", "prompt"), check_vma=False
    )
```
